128 devices in a mesh: row: 4 (over x_lo, core), col: 32 (over z, x_hi, y).
Axes of the slice: x: 4 (x_hi: 2, x_lo: 2; x = x_hi * 2 + x_lo), y: 4, z: 4, core: 2. Of those that a mesh axis runs over, the one named last changes fastest.
Arguments:
- schur: float32 [4096, 16384], P('row', 'col'), may hold values from -6 to 6
- left_rot: float32 [8, 512, 512], P('row', 'col'), may hold values from -1 to 1, as said below
- right_rot: float32 [32, 512, 512], P('col', 'row'), may hold values from -1 to 1, as said below
- left_off: float32 [8, 512, 512], P('row', 'col'), may hold values from -1 to 1, as said below
- right_off: float32 [32, 512, 512], P('col', 'row'), may hold values from -1 to 1, as said below
Outputs:
- updated: float32 [4096, 16384], P('row', 'col')
The draws below stay inside these ranges and needn't reach their ends.
Inputs may be any that keep to these rules, and one draw needn't show every extreme that they name: `left_rot`: each 512 x 512 block is orthogonal. `right_rot`: each 512 x 512 block is orthogonal. `left_off`: each 512 x 512 block is orthogonal. `right_off`: each 512 x 512 block is orthogonal.
All inputs are finite; a program needn't handle non-finite values.
Results may differ from the reference program's by a relative error of at most 0.00007.
Values sent between devices are 32-bit elements; how exact they have to be, the bound alone decides.
No kernel may reach another device: no remote copies, remote signals or barrier semaphores. Data moves between devices by JAX's collectives and lax.ppermute only.
A program may use at most 64 MiB of HBM per device.

```python
import jax
import jax.numpy as jnp
from jax import lax

WIN = 512
NROWS = 4096
NCOLS = 16384
LEFT_WINS = 8
RIGHT_WINS = 32


def orthogonal_blocks(key, number):
    base = jax.random.normal(key, (number, WIN, WIN), jnp.float32)
    factor_q, factor_r = jnp.linalg.qr(base)
    signs = jnp.sign(jnp.diagonal(factor_r, axis1=1, axis2=2)) + 0.0
    signs = jnp.where(signs == 0.0, 1.0, signs)
    return factor_q * signs[:, None, :]


def draw_left_rot(key, part):
    return orthogonal_blocks(jax.random.fold_in(key, 11), LEFT_WINS)


def draw_right_rot(key, part):
    return orthogonal_blocks(jax.random.fold_in(key, 23), RIGHT_WINS)


def draw_left_off(key, part):
    return orthogonal_blocks(jax.random.fold_in(key, 37), LEFT_WINS)


def draw_right_off(key, part):
    return orthogonal_blocks(jax.random.fold_in(key, 41), RIGHT_WINS)


def shard_levels(own_key, extent, cuts, low, top_value):
    level = 1.0
    for axis_at, blocks in cuts:
        draws = jax.random.uniform(jax.random.fold_in(jax.random.fold_in(own_key, 6), axis_at), (blocks,), jnp.float32, low / len(cuts), top_value / len(cuts))
        level = level * jnp.repeat(jnp.exp(draws), extent[axis_at] // blocks).reshape((-1,) + (1,) * (len(extent) - 1 - axis_at))
    return level


def noise(key, shape, deviation, limit, pieces=(), held_as=jnp.bfloat16):
    entries = deviation * jax.random.normal(key, shape, jnp.float32)
    if pieces:
        entries = entries * shard_levels(key, shape, pieces, -0.22, 0.18)
    return jnp.clip(entries, -limit, limit).astype(held_as)


def setup_inputs(seed: int = 0) -> dict:
    key_of = jax.random.split(jax.random.key(seed), 6)
    schur = noise(key_of[0], (NROWS, NCOLS), 1.0, 6.0, ((0, 4), (1, 32)), jnp.float32)
    left_rot = draw_left_rot(jax.random.fold_in(key_of[5], 71), 0)
    right_rot = draw_right_rot(jax.random.fold_in(key_of[5], 71), 0)
    left_off = draw_left_off(jax.random.fold_in(key_of[5], 71), 0)
    right_off = draw_right_off(jax.random.fold_in(key_of[5], 71), 0)
    return {"schur": schur, "left_rot": left_rot, "right_rot": right_rot, "left_off": left_off, "right_off": right_off}


def left_apply(matrix, rotations):
    number = rotations.shape[0]
    window = rotations.shape[1]
    shaped = matrix.reshape(number, window, matrix.shape[1])
    result = jnp.einsum('kab,kac->kbc', rotations, shaped, precision=lax.Precision.HIGHEST)
    return result.reshape(matrix.shape)

def right_apply(matrix, rotations):
    number = rotations.shape[0]
    window = rotations.shape[1]
    shaped = matrix.reshape(matrix.shape[0], number, window)
    result = jnp.einsum('rka,kab->rkb', shaped, rotations, precision=lax.Precision.HIGHEST)
    return result.reshape(matrix.shape)

def reference(schur, left_rot, right_rot, left_off, right_off):
    half_window = WIN // 2
    matrix = left_apply(schur, left_rot)
    matrix = right_apply(matrix, right_rot)
    matrix = jnp.roll(matrix, half_window, axis=0)
    matrix = left_apply(matrix, left_off)
    matrix = jnp.roll(matrix, -half_window, axis=0)
    matrix = jnp.roll(matrix, half_window, axis=1)
    matrix = right_apply(matrix, right_off)
    matrix = jnp.roll(matrix, -half_window, axis=1)
    return matrix
```

```python
import functools

import jax
import jax.numpy as jnp
from jax import lax
from jax.experimental import pallas as pl
from jax.experimental.pallas import tpu as pltpu
from jax.sharding import PartitionSpec as P

WIN = 512
HALF = 256
F32 = jnp.float32
BF16 = jnp.bfloat16


def xor_perm(axis, mask):
    return [(i, i ^ mask) for i in range(lax.axis_size(axis))]


def shift_perm(axis, by):
    size = lax.axis_size(axis)
    return [(i, (i + by) % size) for i in range(size)]


def swap(x, axis, mask):
    return lax.ppermute(x, axis, xor_perm(axis, mask))


def shift(x, axis, by):
    return lax.ppermute(x, axis, shift_perm(axis, by))


def split(x):
    hi = x.astype(BF16)
    lo = (x - hi.astype(F32)).astype(BF16)
    return hi, lo


def dot3(a, b, dims):
    dn = (dims, ((), ()))
    ah, al = a
    bh, bl = b
    dot = functools.partial(lax.dot_general, dimension_numbers=dn, preferred_element_type=F32)
    return dot(ah, bh) + (dot(ah, bl) + dot(al, bh))


NN = ((1,), (0,))
TN = ((0,), (0,))


def place_right(pieces, hi, lo):
    me = lax.axis_index("row")
    for k, piece in enumerate(pieces):
        rows = pl.ds(pl.multiple_of((me ^ k) * 128, 128), 128)
        h, l = split(piece[...])
        hi[rows, :] = h
        lo[rows, :] = l


def place_left(pieces, hi, lo):
    me = lax.axis_index("col")
    for kz, piece in enumerate(pieces):
        for j in range(4):
            for a in range(2):
                at = (me ^ (kz * 8 + a * 4 + j)) * 16
                rows = pl.ds(pl.multiple_of(at, 16), 16)
                h, l = split(piece[(j * 2 + a) * 16 : (j * 2 + a + 1) * 16, :])
                hi[rows, :] = h
                lo[rows, :] = l


def right_aligned(s, p0, p1, p2, p3, ml, mr, qh, ql):
    place_right((p0, p1, p2, p3), qh, ql)
    q = (qh[...], ql[...])
    m = dot3(split(s[...]), q, NN)
    ml[...] = m[:, :HALF]
    mr[...] = m[:, HALF:]


def right_shifted(ml, mr, hl, hr, p0, p1, p2, p3, out, qh, ql):
    place_right((p0, p1, p2, p3), qh, ql)
    for c, (u, v) in enumerate(((hl, ml), (mr, hr))):
        cols = slice(c * HALF, (c + 1) * HALF)
        top = (qh[:HALF, cols], ql[:HALF, cols])
        low = (qh[HALF:, cols], ql[HALF:, cols])
        out[:, cols] = dot3(split(u[...]), top, NN) + dot3(split(v[...]), low, NN)


def left_aligned(x, p0, p1, p2, p3, top, mid, low, qh, ql):
    place_left((p0, p1, p2, p3), qh, ql)
    for k in range(2):
        cols = slice(k * WIN, (k + 1) * WIN)
        n = dot3((qh[:, cols], ql[:, cols]), split(x[cols, :]), TN)
        if k == 0:
            top[...] = n[:HALF]
            mid[:HALF, :] = n[HALF:]
        else:
            mid[HALF:, :] = n[:HALF]
            low[...] = n[HALF:]


def left_shifted(top, mid, low, above, below, p0, p1, p2, p3, out, qh, ql):
    place_left((p0, p1, p2, p3), qh, ql)

    def q(rows, cols):
        return qh[rows, cols], ql[rows, cols]

    first, second = slice(0, HALF), slice(HALF, WIN)
    a, b, c = slice(0, HALF), slice(HALF, HALF + WIN), slice(HALF + WIN, 2 * WIN)
    out[a, :] = dot3(q(first, a), split(above[...]), TN) + dot3(q(second, a), split(top[...]), TN)
    out[b, :] = dot3(q(slice(None), b), split(mid[...]), TN)
    out[c, :] = dot3(q(first, c), split(low[...]), TN) + dot3(q(second, c), split(below[...]), TN)


def kernel_call(kernel, outs, scratch, flops, *args):
    bytes_moved = sum(4 * x.size for x in args) + sum(4 * a * b for a, b in outs)
    return pl.pallas_call(
        kernel,
        out_shape=tuple(jax.ShapeDtypeStruct(s, F32) for s in outs),
        in_specs=[pl.BlockSpec(memory_space=pltpu.VMEM)] * len(args),
        out_specs=tuple(pl.BlockSpec(memory_space=pltpu.VMEM) for _ in outs),
        scratch_shapes=[pltpu.VMEM(scratch, BF16), pltpu.VMEM(scratch, BF16)],
        compiler_params=pltpu.CompilerParams(vmem_limit_bytes=40 * 2**20),
        cost_estimate=pl.CostEstimate(flops=flops, bytes_accessed=bytes_moved, transcendentals=0),
    )(*args)


FLOPS = 3 * 2 * 1024 * 512 * 512


def gather_right(x):
    across = swap(x, "row", 2)
    core = swap(x, "row", 1)
    return x, core, across, swap(across, "row", 1)


def gather_left(x):
    x = jnp.concatenate([x, swap(x, "col", 4)], axis=0)
    x = jnp.concatenate([x] + [swap(x, "col", k) for k in (1, 2, 3)], axis=0)
    return [x] + [swap(x, "col", k * 8) for k in (1, 2, 3)]


def body(schur, left_rot, right_rot, left_off, right_off):
    r1 = gather_right(right_rot[0])
    l1 = gather_left(jnp.concatenate([left_rot[0], left_rot[1]], axis=1))
    ml, mr = kernel_call(right_aligned, [(1024, HALF)] * 2, (WIN, WIN), FLOPS, schur, *r1)
    hl = shift(mr, "col", 1)
    hr = shift(ml, "col", -1)
    following = shift(right_off[0][:, :HALF], "col", -1)
    r2 = gather_right(jnp.concatenate([right_off[0][:, HALF:], following], axis=1))
    following = shift(left_off[0][:, :HALF], "row", -1)
    l2 = gather_left(jnp.concatenate([left_off[0][:, HALF:], left_off[1], following], axis=1))
    (x,) = kernel_call(right_shifted, [(1024, WIN)], (WIN, WIN), FLOPS, ml, mr, hl, hr, *r2)
    top, mid, low = kernel_call(
        left_aligned, [(HALF, WIN), (WIN, WIN), (HALF, WIN)], (WIN, 2 * WIN), FLOPS, x, *l1
    )
    above = shift(low, "row", 1)
    below = shift(top, "row", -1)
    (out,) = kernel_call(
        left_shifted, [(1024, WIN)], (WIN, 2 * WIN), FLOPS, top, mid, low, above, below, *l2
    )
    return out


def solution(mesh):
    return jax.shard_map(
        body,
        mesh=mesh,
        in_specs=(
            P("row", "col"),
            P("row", "col", None),
            P("col", "row", None),
            P("row", "col", None),
            P("col", "row", None),
        ),
        out_specs=P("row", "col"),
        check_vma=False,
    )
```

```python
import functools

import jax
import jax.numpy as jnp
from jax import lax
from jax.experimental import pallas as pl
from jax.experimental.pallas import tpu as pltpu
from jax.sharding import PartitionSpec as P

WIN = 512
HALF = 256
F32 = jnp.float32
BF16 = jnp.bfloat16


def xor_perm(axis, mask):
    return [(i, i ^ mask) for i in range(lax.axis_size(axis))]


def shift_perm(axis, by):
    size = lax.axis_size(axis)
    return [(i, (i + by) % size) for i in range(size)]


def swap(x, axis, mask):
    return lax.ppermute(x, axis, xor_perm(axis, mask))


def shift(x, axis, by):
    return lax.ppermute(x, axis, shift_perm(axis, by))


def split(x):
    hi = x.astype(BF16)
    lo = (x - hi.astype(F32)).astype(BF16)
    return hi, lo


def dot3(a, b, dims):
    dn = (dims, ((), ()))
    ah, al = a
    bh, bl = b
    dot = functools.partial(lax.dot_general, dimension_numbers=dn, preferred_element_type=F32)
    return dot(ah, bh) + (dot(ah, bl) + dot(al, bh))


NN = ((1,), (0,))
TN = ((0,), (0,))


def place_right(own, core, cols, place, hi, lo):
    me = lax.axis_index("row")
    for mask, source, at in ((0, own, 0), (2, own, 128), (1, core, 0), (3, core, 128)):
        rows = pl.ds(pl.multiple_of((me ^ mask) * 128, 128), 128)
        h, l = split(source[at : at + 128, cols])
        hi[rows, place] = h
        lo[rows, place] = l


def place_left(pieces, hi, lo):
    z = lax.axis_index("col") // 8
    own, up, down, far_first, far_second = pieces
    for by, at, source in ((0, 0, own), (3, 0, up), (1, 0, down), (2, 0, far_first), (2, 64, far_second)):
        size = source.shape[0]
        rows = pl.ds(pl.multiple_of((z + by) % 4 * 128 + at, size), size)
        h, l = split(source[...])
        hi[rows, :] = h
        lo[rows, :] = l


def right_aligned(s, own, core, *rest):
    ml, mr, rows, qh, ql, sems = rest[-6:]
    tile = rows.shape[0] // sems.shape[0]
    tiles = [slice(k * tile, (k + 1) * tile) for k in range(sems.shape[0])]
    reads = [pltpu.make_async_copy(s.at[t], rows.at[t], sems.at[k]) for k, t in enumerate(tiles)]
    for read in reads:
        read.start()
    place_right(own, core, slice(0, WIN), slice(0, WIN), qh, ql)
    for t, read in zip(tiles, reads):
        read.wait()
        m = dot3(split(rows[t, :]), (qh[...], ql[...]), NN)
        ml[t, :] = m[:, :HALF]
        mr[t, :] = m[:, HALF:]


def middle(ml, mr, hl, hr, own, core, next_own, next_core, p0, p1, p2, p3, p4, *rest):
    top, mid, low, x, qh, ql, lh, ll = rest[-8:]
    place_right(own, core, slice(WIN, WIN + HALF), slice(0, HALF), qh, ql)
    place_right(next_own, next_core, slice(0, HALF), slice(HALF, WIN), qh, ql)
    for c, (u, v) in enumerate(((hl, ml), (mr, hr))):
        cols = slice(c * HALF, (c + 1) * HALF)
        first = (qh[:HALF, cols], ql[:HALF, cols])
        second = (qh[HALF:, cols], ql[HALF:, cols])
        x[:, cols] = dot3(split(u[...]), first, NN) + dot3(split(v[...]), second, NN)
    place_left((p0, p1, p2, p3, p4), lh, ll)
    for k in range(2):
        cols = slice(k * WIN, (k + 1) * WIN)
        n = dot3((lh[:, cols], ll[:, cols]), split(x[cols, :]), TN)
        if k == 0:
            top[...] = n[:HALF]
            mid[:HALF, :] = n[HALF:]
        else:
            mid[HALF:, :] = n[:HALF]
            low[...] = n[HALF:]


def left_shifted(top, mid, low, above, below, p0, p1, p2, p3, p4, out, y, qh, ql, sems):
    place_left((p0, p1, p2, p3, p4), qh, ql)

    def q(rows, cols):
        return qh[rows, cols], ql[rows, cols]

    def write(part, k):
        copy = pltpu.make_async_copy(y.at[part], out.at[part], sems.at[k])
        copy.start()
        return copy

    first, second = slice(0, HALF), slice(HALF, WIN)
    a, b, c = slice(0, HALF), slice(HALF, HALF + WIN), slice(HALF + WIN, 2 * WIN)
    y[b, :] = dot3(q(slice(None), b), split(mid[...]), TN)
    writes = [write(b, 0)]
    y[a, :] = dot3(q(first, a), split(above[...]), TN) + dot3(q(second, a), split(top[...]), TN)
    writes.append(write(a, 1))
    y[c, :] = dot3(q(first, c), split(low[...]), TN) + dot3(q(second, c), split(below[...]), TN)
    writes.append(write(c, 2))
    for copy in writes:
        copy.wait()


LAST = "y"
FLOPS = 3 * 2 * 1024 * 512 * 512
ANY = pl.BlockSpec(memory_space=pl.ANY)
HBM = pl.BlockSpec(memory_space=pltpu.HBM)
VMEM = pl.BlockSpec(memory_space=pltpu.VMEM)
EVERY = slice(None)


def call(kernel, outs, args, specs, scratch, flops, mib, vmem, out_spec=VMEM):
    return pl.pallas_call(
        kernel,
        out_shape=tuple(jax.ShapeDtypeStruct(s, F32) for s in outs),
        in_specs=specs,
        out_specs=(out_spec,) * len(outs),
        scratch_shapes=scratch,
        compiler_params=pltpu.CompilerParams(vmem_limit_bytes=vmem * 2**20),
        cost_estimate=pl.CostEstimate(flops=flops, bytes_accessed=mib * 2**20, transcendentals=0),
    )(*args)


def joined(outs, args, copies, after=()):
    n, m = len(args), len(after)

    def kernel(*refs):
        for source, part, target, place in copies:
            refs[n + m + target][place] = refs[source][part]

    return call(kernel, outs, (*args, *after), [VMEM] * n + [ANY] * m, [], 0, 1, 4)


def stacked(pieces, after=()):
    size, width = pieces[0].shape
    copies = [
        (k, (EVERY, EVERY), 0, (slice(k * size, (k + 1) * size), EVERY)) for k in range(len(pieces))
    ]
    return joined([(len(pieces) * size, width)], pieces, copies, after)[0]


def first_right(schur, pieces, after):
    shape = schur.shape
    half = (shape[0], HALF)
    scratch = [pltpu.VMEM(shape, F32)] + [pltpu.VMEM((WIN, WIN), BF16)] * 2
    scratch.append(pltpu.SemaphoreType.DMA((4,)))
    specs = [HBM] + [VMEM] * 2 + [ANY] * len(after)
    return call(right_aligned, [half, half], (schur, *pieces, *after), specs, scratch, FLOPS, 5, 12)


def middle_products(parts, r2, l1, after):
    args = (*parts, *r2, *l1)
    scratch = [pltpu.VMEM((2 * WIN, WIN), F32)]
    scratch += [pltpu.VMEM((WIN, WIN), BF16)] * 2 + [pltpu.VMEM((WIN, 2 * WIN), BF16)] * 2
    outs = [(HALF, WIN), (WIN, WIN), (HALF, WIN)]
    specs = [VMEM] * len(args) + [ANY] * len(after)
    return call(middle, outs, (*args, *after), specs, scratch, 2 * FLOPS, 9, 20)


def last_left(parts, l2):
    scratch = [pltpu.VMEM((2 * WIN, WIN), F32)] + [pltpu.VMEM((WIN, 2 * WIN), BF16)] * 2
    scratch.append(pltpu.SemaphoreType.DMA((3,)))
    args = (*parts, *l2)
    outs = [(2 * WIN, WIN)]
    return call(left_shifted, outs, args, [VMEM] * len(args), scratch, FLOPS, 7, 20, HBM)[0]


def gathered(x):
    size = 8
    groups = [[z * size + i for i in range(size)] for z in range(lax.axis_size("col") // size)]
    copies = jnp.broadcast_to(x[None], (size,) + x.shape)
    out = lax.all_to_all(copies, "col", 0, 0, axis_index_groups=groups)
    return out.reshape(size * x.shape[0], x.shape[1])


def ring(x, to):
    perm = [(i, to(i)) for i in range(lax.axis_size("col"))]
    return lax.ppermute(x, "col", perm)


def along_z(by):
    return lambda i: (i + 8 * by) % 32


def around(x, along):
    up = ring(x, along(1))
    down = ring(x, along(-1))
    return x, up, down, ring(up[:64], along(1)), ring(down[64:], along(-1))


def body(schur, left_rot, right_rot, left_off, right_off):
    right = jnp.concatenate([right_rot[0], right_off[0, :, HALF:]], axis=1)
    right = stacked([right, swap(right, "row", 2)])
    right_next = shift(right_off[0, :, :HALF], "col", -1)
    left = gathered(jnp.concatenate([left_rot[0], left_rot[1], left_off[0], left_off[1]], axis=1))
    l1, l2_away, l2 = joined(
        [(128, 2 * WIN), (128, HALF), (128, 2 * WIN - HALF)],
        [left],
        [
            (0, (EVERY, slice(0, 2 * WIN)), 0, (EVERY, EVERY)),
            (0, (EVERY, slice(2 * WIN, 2 * WIN + HALF)), 1, (EVERY, EVERY)),
            (0, (EVERY, slice(2 * WIN + HALF, 4 * WIN)), 2, (EVERY, EVERY)),
        ],
        after=(right_next, right),
    )
    right_core = swap(right, "row", 1)
    right_next = stacked([right_next, swap(right_next, "row", 2)])
    ml, mr = first_right(schur, (right, right_core), (l1,))
    hl = shift(mr, "col", 1)
    hr = shift(ml, "col", -1)
    l1 = around(l1, along_z)
    (l2,) = joined(
        [(128, 2 * WIN)],
        [l2, shift(l2_away, "row", -1)],
        [
            (0, (EVERY, EVERY), 0, (EVERY, slice(0, 2 * WIN - HALF))),
            (1, (EVERY, EVERY), 0, (EVERY, slice(2 * WIN - HALF, 2 * WIN))),
        ],
    )
    next_core = swap(right_next, "row", 1)
    top, mid, low = middle_products(
        (ml, mr, hl, hr), (right, right_core, right_next, next_core), l1, ()
    )
    l2 = around(l2, along_z)
    above = shift(low, "row", 1)
    below = shift(top, "row", -1)
    return last_left((top, mid, low, above, below), l2)


def solution(mesh):
    return jax.shard_map(
        body,
        mesh=mesh,
        in_specs=(
            P("row", "col"),
            P("row", "col", None),
            P("col", "row", None),
            P("row", "col", None),
            P("col", "row", None),
        ),
        out_specs=P("row", "col"),
        check_vma=False,
    )
```

```python
import functools

import jax
import jax.numpy as jnp
from jax import lax
from jax.experimental import pallas as pl
from jax.experimental.pallas import tpu as pltpu
from jax.sharding import PartitionSpec as P

WIN = 512
HALF = 256
F32 = jnp.float32
BF16 = jnp.bfloat16


def xor_perm(axis, mask):
    return [(i, i ^ mask) for i in range(lax.axis_size(axis))]


def shift_perm(axis, by):
    size = lax.axis_size(axis)
    return [(i, (i + by) % size) for i in range(size)]


def swap(x, axis, mask):
    return lax.ppermute(x, axis, xor_perm(axis, mask))


def shift(x, axis, by):
    return lax.ppermute(x, axis, shift_perm(axis, by))


def split(x):
    hi = x.astype(BF16)
    lo = (x - hi.astype(F32)).astype(BF16)
    return hi, lo


def dot3(a, b, dims):
    dn = (dims, ((), ()))
    ah, al = a
    bh, bl = b
    dot = functools.partial(lax.dot_general, dimension_numbers=dn, preferred_element_type=F32)
    return dot(ah, bh) + (dot(ah, bl) + dot(al, bh))


NN = ((1,), (0,))
TN = ((0,), (0,))


def place_right(own, core, cols, place, hi, lo):
    me = lax.axis_index("row")
    for mask, source, at in ((0, own, 0), (2, own, 128), (1, core, 0), (3, core, 128)):
        rows = pl.ds(pl.multiple_of((me ^ mask) * 128, 128), 128)
        h, l = split(source[at : at + 128, cols])
        hi[rows, place] = h
        lo[rows, place] = l


def place_left(pieces, hi, lo):
    z = lax.axis_index("col") // 8
    own, up, down, far_first, far_second = pieces
    for by, at, source in ((0, 0, own), (3, 0, up), (1, 0, down), (2, 0, far_first), (2, 64, far_second)):
        size = source.shape[0]
        rows = pl.ds(pl.multiple_of((z + by) % 4 * 128 + at, size), size)
        h, l = split(source[...])
        hi[rows, :] = h
        lo[rows, :] = l


def right_aligned(s, own, core, *rest):
    ml, mr, rows, qh, ql, sems = rest[-6:]
    tile = rows.shape[0] // sems.shape[0]
    tiles = [slice(k * tile, (k + 1) * tile) for k in range(sems.shape[0])]
    reads = [pltpu.make_async_copy(s.at[t], rows.at[t], sems.at[k]) for k, t in enumerate(tiles)]
    for read in reads:
        read.start()
    place_right(own, core, slice(0, WIN), slice(0, WIN), qh, ql)
    for t, read in zip(tiles, reads):
        read.wait()
        m = dot3(split(rows[t, :]), (qh[...], ql[...]), NN)
        ml[t, :] = m[:, :HALF]
        mr[t, :] = m[:, HALF:]


def middle(ml, mr, hl, hr, own, core, next_own, next_core, p0, p1, p2, p3, p4, *rest):
    top, mid, low, x, qh, ql, lh, ll = rest[-8:]
    place_right(own, core, slice(WIN, WIN + HALF), slice(0, HALF), qh, ql)
    place_right(next_own, next_core, slice(0, HALF), slice(HALF, WIN), qh, ql)
    for c, (u, v) in enumerate(((hl, ml), (mr, hr))):
        cols = slice(c * HALF, (c + 1) * HALF)
        first = (qh[:HALF, cols], ql[:HALF, cols])
        second = (qh[HALF:, cols], ql[HALF:, cols])
        x[:, cols] = dot3(split(u[...]), first, NN) + dot3(split(v[...]), second, NN)
    place_left((p0, p1, p2, p3, p4), lh, ll)
    for k in range(2):
        cols = slice(k * WIN, (k + 1) * WIN)
        n = dot3((lh[:, cols], ll[:, cols]), split(x[cols, :]), TN)
        if k == 0:
            top[...] = n[:HALF]
            mid[:HALF, :] = n[HALF:]
        else:
            mid[HALF:, :] = n[:HALF]
            low[...] = n[HALF:]


def left_shifted(top, mid, low, above, below, p0, p1, p2, p3, p4, out, y, qh, ql, sems):
    place_left((p0, p1, p2, p3, p4), qh, ql)

    def q(rows, cols):
        return qh[rows, cols], ql[rows, cols]

    def write(part, k):
        copy = pltpu.make_async_copy(y.at[part], out.at[part], sems.at[k])
        copy.start()
        return copy

    first, second = slice(0, HALF), slice(HALF, WIN)
    a, b, c = slice(0, HALF), slice(HALF, HALF + WIN), slice(HALF + WIN, 2 * WIN)
    y[b, :] = dot3(q(slice(None), b), split(mid[...]), TN)
    writes = [write(b, 0)]
    y[a, :] = dot3(q(first, a), split(above[...]), TN) + dot3(q(second, a), split(top[...]), TN)
    writes.append(write(a, 1))
    y[c, :] = dot3(q(first, c), split(low[...]), TN) + dot3(q(second, c), split(below[...]), TN)
    writes.append(write(c, 2))
    for copy in writes:
        copy.wait()


LAST = "y"
FLOPS = 3 * 2 * 1024 * 512 * 512
ANY = pl.BlockSpec(memory_space=pl.ANY)
HBM = pl.BlockSpec(memory_space=pltpu.HBM)
VMEM = pl.BlockSpec(memory_space=pltpu.VMEM)
EVERY = slice(None)


def call(kernel, outs, args, specs, scratch, flops, mib, vmem, out_spec=VMEM):
    return pl.pallas_call(
        kernel,
        out_shape=tuple(jax.ShapeDtypeStruct(s, F32) for s in outs),
        in_specs=specs,
        out_specs=(out_spec,) * len(outs),
        scratch_shapes=scratch,
        compiler_params=pltpu.CompilerParams(vmem_limit_bytes=vmem * 2**20),
        cost_estimate=pl.CostEstimate(flops=flops, bytes_accessed=mib * 2**20, transcendentals=0),
    )(*args)


def joined(outs, args, copies, after=()):
    n, m = len(args), len(after)

    def kernel(*refs):
        for source, part, target, place in copies:
            refs[n + m + target][place] = refs[source][part]

    return call(kernel, outs, (*args, *after), [VMEM] * n + [ANY] * m, [], 0, 1, 4)


def stacked(pieces, after=()):
    size, width = pieces[0].shape
    copies = [
        (k, (EVERY, EVERY), 0, (slice(k * size, (k + 1) * size), EVERY)) for k in range(len(pieces))
    ]
    return joined([(len(pieces) * size, width)], pieces, copies, after)[0]


def first_right(schur, pieces, after):
    shape = schur.shape
    half = (shape[0], HALF)
    scratch = [pltpu.VMEM(shape, F32)] + [pltpu.VMEM((WIN, WIN), BF16)] * 2
    scratch.append(pltpu.SemaphoreType.DMA((4,)))
    specs = [HBM] + [VMEM] * 2 + [ANY] * len(after)
    return call(right_aligned, [half, half], (schur, *pieces, *after), specs, scratch, FLOPS, 5, 12)


def middle_products(parts, r2, l1, after):
    args = (*parts, *r2, *l1)
    scratch = [pltpu.VMEM((2 * WIN, WIN), F32)]
    scratch += [pltpu.VMEM((WIN, WIN), BF16)] * 2 + [pltpu.VMEM((WIN, 2 * WIN), BF16)] * 2
    outs = [(HALF, WIN), (WIN, WIN), (HALF, WIN)]
    specs = [VMEM] * len(args) + [ANY] * len(after)
    return call(middle, outs, (*args, *after), specs, scratch, 2 * FLOPS, 9, 20)


def last_left(parts, l2):
    scratch = [pltpu.VMEM((2 * WIN, WIN), F32)] + [pltpu.VMEM((WIN, 2 * WIN), BF16)] * 2
    scratch.append(pltpu.SemaphoreType.DMA((3,)))
    args = (*parts, *l2)
    outs = [(2 * WIN, WIN)]
    return call(left_shifted, outs, args, [VMEM] * len(args), scratch, FLOPS, 7, 20, HBM)[0]


def across_next(x):
    rows, cols = lax.axis_size("row"), lax.axis_size("col")
    perm = [(r * cols + c, (r ^ 2) * cols + (c - 1) % cols) for r in range(rows) for c in range(cols)]
    return lax.ppermute(x, ("row", "col"), perm)


def gathered(x):
    size = 8
    groups = [[z * size + i for i in range(size)] for z in range(lax.axis_size("col") // size)]
    copies = jnp.broadcast_to(x[None], (size,) + x.shape)
    out = lax.all_to_all(copies, "col", 0, 0, axis_index_groups=groups)
    return out.reshape(size * x.shape[0], x.shape[1])


def ring(x, to):
    perm = [(i, to(i)) for i in range(lax.axis_size("col"))]
    return lax.ppermute(x, "col", perm)


def along_z(by):
    return lambda i: (i + 8 * by) % 32


def around(x, along):
    up = ring(x, along(1))
    down = ring(x, along(-1))
    return x, up, down, ring(up[:64], along(1)), ring(down[64:], along(-1))


def body(schur, left_rot, right_rot, left_off, right_off):
    l1 = gathered(jnp.concatenate([left_rot[0], left_rot[1]], axis=1))
    l1 = around(l1, along_z)
    right_next = right_off[0, :, :HALF]
    right_next = stacked([shift(right_next, "col", -1), across_next(right_next)])
    away = shift(left_off[0, :, :HALF], "row", -1)
    l2 = jnp.concatenate([left_off[0, :, HALF:], left_off[1]], axis=1)
    (l2,) = joined(
        [(16, 2 * WIN)],
        [l2, away],
        [
            (0, (EVERY, EVERY), 0, (EVERY, slice(0, 2 * WIN - HALF))),
            (1, (EVERY, EVERY), 0, (EVERY, slice(2 * WIN - HALF, 2 * WIN))),
        ],
        after=(right_next,),
    )
    l2 = gathered(l2)
    right = jnp.concatenate([right_rot[0], right_off[0, :, HALF:]], axis=1)
    right = stacked([right, swap(right, "row", 2)])
    right_core = swap(right, "row", 1)
    ml, mr = first_right(schur, (right, right_core), (l2, l1[1], l1[2]))
    hl = shift(mr, "col", 1)
    hr = shift(ml, "col", -1)
    next_core = swap(right_next, "row", 1)
    top, mid, low = middle_products(
        (ml, mr, hl, hr), (right, right_core, right_next, next_core), l1, ()
    )
    l2 = around(l2, along_z)
    above = shift(low, "row", 1)
    below = shift(top, "row", -1)
    return last_left((top, mid, low, above, below), l2)


def solution(mesh):
    return jax.shard_map(
        body,
        mesh=mesh,
        in_specs=(
            P("row", "col"),
            P("row", "col", None),
            P("col", "row", None),
            P("row", "col", None),
            P("col", "row", None),
        ),
        out_specs=P("row", "col"),
        check_vma=False,
    )
```

```python
import functools

import jax
import jax.numpy as jnp
from jax import lax
from jax.experimental import pallas as pl
from jax.experimental.pallas import tpu as pltpu
from jax.sharding import PartitionSpec as P

WIN = 512
HALF = 256
F32 = jnp.float32
BF16 = jnp.bfloat16


def xor_perm(axis, mask):
    return [(i, i ^ mask) for i in range(lax.axis_size(axis))]


def shift_perm(axis, by):
    size = lax.axis_size(axis)
    return [(i, (i + by) % size) for i in range(size)]


def swap(x, axis, mask):
    return lax.ppermute(x, axis, xor_perm(axis, mask))


def shift(x, axis, by):
    return lax.ppermute(x, axis, shift_perm(axis, by))


def split(x):
    hi = x.astype(BF16)
    lo = (x - hi.astype(F32)).astype(BF16)
    return hi, lo


def dot3(a, b, dims):
    dn = (dims, ((), ()))
    ah, al = a
    bh, bl = b
    dot = functools.partial(lax.dot_general, dimension_numbers=dn, preferred_element_type=F32)
    return dot(ah, bh) + (dot(ah, bl) + dot(al, bh))


NN = ((1,), (0,))
TN = ((0,), (0,))


def place_right(own, core, cols, place, hi, lo):
    me = lax.axis_index("row")
    for mask, source, at in ((0, own, 0), (2, own, 128), (1, core, 0), (3, core, 128)):
        rows = pl.ds(pl.multiple_of((me ^ mask) * 128, 128), 128)
        h, l = split(source[at : at + 128, cols])
        hi[rows, place] = h
        lo[rows, place] = l


def place_left(placed, hi, lo):
    z = lax.axis_index("col") // 8
    for by, at, source in placed:
        size = source.shape[0]
        rows = pl.ds(pl.multiple_of((z + by) % 4 * 128 + at, size), size)
        h, l = split(source[...])
        hi[rows, :] = h
        lo[rows, :] = l


def right_aligned(s, own, core, *rest):
    ml, mr, rows, qh, ql, sems = rest[-6:]
    tile = rows.shape[0] // sems.shape[0]
    tiles = [slice(k * tile, (k + 1) * tile) for k in range(sems.shape[0])]
    reads = [pltpu.make_async_copy(s.at[t], rows.at[t], sems.at[k]) for k, t in enumerate(tiles)]
    for read in reads:
        read.start()
    place_right(own, core, slice(0, WIN), slice(0, WIN), qh, ql)
    for t, read in zip(tiles, reads):
        read.wait()
        m = dot3(split(rows[t, :]), (qh[...], ql[...]), NN)
        ml[t, :] = m[:, :HALF]
        mr[t, :] = m[:, HALF:]


def prepare(ml, mr, own, core, next_own, next_core, p0, p1, p2, x, ah, al, lh, ll, qh, ql):
    place_right(own, core, slice(WIN, WIN + HALF), slice(0, HALF), qh, ql)
    place_right(next_own, next_core, slice(0, HALF), slice(HALF, WIN), qh, ql)
    first, second = slice(0, HALF), slice(HALF, WIN)
    x[:, first] = dot3(split(ml[...]), (qh[second, first], ql[second, first]), NN)
    x[:, second] = dot3(split(mr[...]), (qh[first, second], ql[first, second]), NN)
    for to, part in ((ah, qh), (al, ql)):
        to[:, first] = part[first, first]
        to[:, second] = part[second, second]
    place_left(((0, 0, p0), (3, 0, p1), (1, 0, p2)), lh, ll)


def middle(hl, hr, own, ah, al, near_h, near_l, p3, p4, top, mid, low, x, lh, ll):
    lh[...] = near_h[...]
    ll[...] = near_l[...]
    place_left(((2, 0, p3), (2, 64, p4)), lh, ll)
    for c, u in enumerate((hl, hr)):
        cols = slice(c * HALF, (c + 1) * HALF)
        x[:, cols] = own[:, cols] + dot3(split(u[...]), (ah[:, cols], al[:, cols]), NN)
    for k in range(2):
        cols = slice(k * WIN, (k + 1) * WIN)
        n = dot3((lh[:, cols], ll[:, cols]), split(x[cols, :]), TN)
        if k == 0:
            top[...] = n[:HALF]
            mid[:HALF, :] = n[HALF:]
        else:
            mid[HALF:, :] = n[:HALF]
            low[...] = n[HALF:]


def left_shifted(top, mid, low, above, below, p0, p1, p2, p3, p4, out, y, qh, ql, sems):
    place_left(((0, 0, p0), (3, 0, p1), (1, 0, p2), (2, 0, p3), (2, 64, p4)), qh, ql)

    def q(rows, cols):
        return qh[rows, cols], ql[rows, cols]

    def write(part, k):
        copy = pltpu.make_async_copy(y.at[part], out.at[part], sems.at[k])
        copy.start()
        return copy

    first, second = slice(0, HALF), slice(HALF, WIN)
    a, b, c = slice(0, HALF), slice(HALF, HALF + WIN), slice(HALF + WIN, 2 * WIN)
    y[b, :] = dot3(q(slice(None), b), split(mid[...]), TN)
    writes = [write(b, 0)]
    y[a, :] = dot3(q(first, a), split(above[...]), TN) + dot3(q(second, a), split(top[...]), TN)
    writes.append(write(a, 1))
    y[c, :] = dot3(q(first, c), split(low[...]), TN) + dot3(q(second, c), split(below[...]), TN)
    writes.append(write(c, 2))
    for copy in writes:
        copy.wait()


LAST = "y"
FLOPS = 3 * 2 * 1024 * 512 * 512
ANY = pl.BlockSpec(memory_space=pl.ANY)
HBM = pl.BlockSpec(memory_space=pltpu.HBM)
VMEM = pl.BlockSpec(memory_space=pltpu.VMEM)
EVERY = slice(None)


def call(kernel, outs, args, specs, scratch, flops, mib, vmem, out_spec=VMEM):
    return pl.pallas_call(
        kernel,
        out_shape=tuple(jax.ShapeDtypeStruct(s, F32) for s in outs),
        in_specs=specs,
        out_specs=(out_spec,) * len(outs),
        scratch_shapes=scratch,
        compiler_params=pltpu.CompilerParams(vmem_limit_bytes=vmem * 2**20),
        cost_estimate=pl.CostEstimate(flops=flops, bytes_accessed=mib * 2**20, transcendentals=0),
    )(*args)


def joined(outs, args, copies, after=()):
    n, m = len(args), len(after)

    def kernel(*refs):
        for source, part, target, place in copies:
            refs[n + m + target][place] = refs[source][part]

    return call(kernel, outs, (*args, *after), [VMEM] * n + [ANY] * m, [], 0, 1, 4)


def stacked(pieces, after=()):
    size, width = pieces[0].shape
    copies = [
        (k, (EVERY, EVERY), 0, (slice(k * size, (k + 1) * size), EVERY)) for k in range(len(pieces))
    ]
    return joined([(len(pieces) * size, width)], pieces, copies, after)[0]


def first_right(schur, pieces, after):
    shape = schur.shape
    half = (shape[0], HALF)
    scratch = [pltpu.VMEM(shape, F32)] + [pltpu.VMEM((WIN, WIN), BF16)] * 2
    scratch.append(pltpu.SemaphoreType.DMA((4,)))
    specs = [HBM] + [VMEM] * 2 + [ANY] * len(after)
    return call(right_aligned, [half, half], (schur, *pieces, *after), specs, scratch, FLOPS, 5, 12)


def prepared(parts, r2, near):
    args = (*parts, *r2, *near)
    outs = [((2 * WIN, WIN), F32)] + [((HALF, WIN), BF16)] * 2 + [((WIN, 2 * WIN), BF16)] * 2
    return pl.pallas_call(
        prepare,
        out_shape=tuple(jax.ShapeDtypeStruct(*o) for o in outs),
        in_specs=[VMEM] * len(args),
        out_specs=(VMEM,) * len(outs),
        scratch_shapes=[pltpu.VMEM((WIN, WIN), BF16)] * 2,
        compiler_params=pltpu.CompilerParams(vmem_limit_bytes=16 * 2**20),
        cost_estimate=pl.CostEstimate(flops=FLOPS // 2, bytes_accessed=7 * 2**20, transcendentals=0),
    )(*args)


def middle_products(parts, ready, far):
    args = (*parts, *ready, *far)
    scratch = [pltpu.VMEM((2 * WIN, WIN), F32)] + [pltpu.VMEM((WIN, 2 * WIN), BF16)] * 2
    outs = [(HALF, WIN), (WIN, WIN), (HALF, WIN)]
    return call(middle, outs, args, [VMEM] * len(args), scratch, 3 * FLOPS // 2, 9, 20)


def last_left(parts, l2):
    scratch = [pltpu.VMEM((2 * WIN, WIN), F32)] + [pltpu.VMEM((WIN, 2 * WIN), BF16)] * 2
    scratch.append(pltpu.SemaphoreType.DMA((3,)))
    args = (*parts, *l2)
    outs = [(2 * WIN, WIN)]
    return call(left_shifted, outs, args, [VMEM] * len(args), scratch, FLOPS, 7, 20, HBM)[0]


def across_next(x):
    rows, cols = lax.axis_size("row"), lax.axis_size("col")
    perm = [(r * cols + c, (r ^ 2) * cols + (c - 1) % cols) for r in range(rows) for c in range(cols)]
    return lax.ppermute(x, ("row", "col"), perm)


def gathered(x):
    size = 8
    groups = [[z * size + i for i in range(size)] for z in range(lax.axis_size("col") // size)]
    copies = jnp.broadcast_to(x[None], (size,) + x.shape)
    out = lax.all_to_all(copies, "col", 0, 0, axis_index_groups=groups)
    return out.reshape(size * x.shape[0], x.shape[1])


def ring(x, to):
    perm = [(i, to(i)) for i in range(lax.axis_size("col"))]
    return lax.ppermute(x, "col", perm)


def along_z(by):
    return lambda i: (i + 8 * by) % 32


def around(x, along):
    up = ring(x, along(1))
    down = ring(x, along(-1))
    return x, up, down, ring(up[:64], along(1)), ring(down[64:], along(-1))


def body(schur, left_rot, right_rot, left_off, right_off):
    l1 = gathered(jnp.concatenate([left_rot[0], left_rot[1]], axis=1))
    l1 = l1, ring(l1, along_z(1)), ring(l1, along_z(-1))
    right_next = right_off[0, :, :HALF]
    right_next = stacked([shift(right_next, "col", -1), across_next(right_next)])
    away = shift(left_off[0, :, :HALF], "row", -1)
    l2 = jnp.concatenate([left_off[0, :, HALF:], left_off[1]], axis=1)
    (l2,) = joined(
        [(16, 2 * WIN)],
        [l2, away],
        [
            (0, (EVERY, EVERY), 0, (EVERY, slice(0, 2 * WIN - HALF))),
            (1, (EVERY, EVERY), 0, (EVERY, slice(2 * WIN - HALF, 2 * WIN))),
        ],
        after=(right_next,),
    )
    l2 = gathered(l2)
    right = jnp.concatenate([right_rot[0], right_off[0, :, HALF:]], axis=1)
    right = stacked([right, swap(right, "row", 2)])
    right_core = swap(right, "row", 1)
    ml, mr = first_right(schur, (right, right_core), (l2, l1[1], l1[2]))
    hl = shift(mr, "col", 1)
    hr = shift(ml, "col", -1)
    next_core = swap(right_next, "row", 1)
    ready = prepared((ml, mr), (right, right_core, right_next, next_core), l1[:3])
    far_first, far_second = joined(
        [(64, 2 * WIN)] * 2,
        [l1[1], l1[2]],
        [(k, (slice(k * 64, k * 64 + 64), EVERY), k, (EVERY, EVERY)) for k in (0, 1)],
        after=(ready[0],),
    )
    far = ring(far_first, along_z(1)), ring(far_second, along_z(-1))
    top, mid, low = middle_products((hl, hr), ready, far)
    l2 = around(l2, along_z)
    above = shift(low, "row", 1)
    below = shift(top, "row", -1)
    return last_left((top, mid, low, above, below), l2)


def solution(mesh):
    return jax.shard_map(
        body,
        mesh=mesh,
        in_specs=(
            P("row", "col"),
            P("row", "col", None),
            P("col", "row", None),
            P("row", "col", None),
            P("col", "row", None),
        ),
        out_specs=P("row", "col"),
        check_vma=False,
    )
```

```python
import functools

import jax
import jax.numpy as jnp
from jax import lax
from jax.experimental import pallas as pl
from jax.experimental.pallas import tpu as pltpu
from jax.sharding import PartitionSpec as P

WIN = 512
HALF = 256
F32 = jnp.float32
BF16 = jnp.bfloat16


def xor_perm(axis, mask):
    return [(i, i ^ mask) for i in range(lax.axis_size(axis))]


def shift_perm(axis, by):
    size = lax.axis_size(axis)
    return [(i, (i + by) % size) for i in range(size)]


def swap(x, axis, mask):
    return lax.ppermute(x, axis, xor_perm(axis, mask))


def shift(x, axis, by):
    return lax.ppermute(x, axis, shift_perm(axis, by))


def split(x):
    hi = x.astype(BF16)
    lo = (x - hi.astype(F32)).astype(BF16)
    return hi, lo


def dot3(a, b, dims):
    dn = (dims, ((), ()))
    ah, al = a
    bh, bl = b
    dot = functools.partial(lax.dot_general, dimension_numbers=dn, preferred_element_type=F32)
    return dot(ah, bh) + (dot(ah, bl) + dot(al, bh))


NN = ((1,), (0,))
TN = ((0,), (0,))


def place_right(own, core, cols, place, hi, lo):
    me = lax.axis_index("row")
    for mask, source, at in ((0, own, 0), (2, own, 128), (1, core, 0), (3, core, 128)):
        rows = pl.ds(pl.multiple_of((me ^ mask) * 128, 128), 128)
        h, l = split(source[at : at + 128, cols])
        hi[rows, place] = h
        lo[rows, place] = l


def place_left(placed, hi, lo):
    z = lax.axis_index("col") // 8
    for by, at, source in placed:
        size = source.shape[0]
        rows = pl.ds(pl.multiple_of((z + by) % 4 * 128 + at, size), size)
        h, l = split(source[...])
        hi[rows, :] = h
        lo[rows, :] = l


def right_aligned(s, own, core, *rest):
    ml, mr, rows, qh, ql, sems = rest[-6:]
    tile = rows.shape[0] // sems.shape[0]
    tiles = [slice(k * tile, (k + 1) * tile) for k in range(sems.shape[0])]
    reads = [pltpu.make_async_copy(s.at[t], rows.at[t], sems.at[k]) for k, t in enumerate(tiles)]
    for read in reads:
        read.start()
    place_right(own, core, slice(0, WIN), slice(0, WIN), qh, ql)
    for t, read in zip(tiles, reads):
        read.wait()
        m = dot3(split(rows[t, :]), (qh[...], ql[...]), NN)
        ml[t, :] = m[:, :HALF]
        mr[t, :] = m[:, HALF:]


def prepare(ml, mr, own, core, next_own, next_core, p0, p1, p2, x, ah, al, lh, ll, qh, ql):
    place_right(own, core, slice(WIN, WIN + HALF), slice(0, HALF), qh, ql)
    place_right(next_own, next_core, slice(0, HALF), slice(HALF, WIN), qh, ql)
    first, second = slice(0, HALF), slice(HALF, WIN)
    x[:, first] = dot3(split(ml[...]), (qh[second, first], ql[second, first]), NN)
    x[:, second] = dot3(split(mr[...]), (qh[first, second], ql[first, second]), NN)
    for to, part in ((ah, qh), (al, ql)):
        to[:, first] = part[first, first]
        to[:, second] = part[second, second]
    place_left(((0, 0, p0), (3, 0, p1), (1, 0, p2)), lh, ll)


def middle(w, hl, hr, own, ah, al, near_h, near_l, p3, p4, first, second, x, lh, ll):
    window = slice(w * WIN, (w + 1) * WIN)
    lh[...] = near_h[:, window]
    ll[...] = near_l[:, window]
    place_left(((2, 0, p3.at[:, window]), (2, 64, p4.at[:, window])), lh, ll)
    for c, u in enumerate((hl, hr)):
        cols = slice(c * HALF, (c + 1) * HALF)
        x[:, cols] = own[window, cols] + dot3(split(u[window, :]), (ah[:, cols], al[:, cols]), NN)
    n = dot3((lh[...], ll[...]), split(x[...]), TN)
    first[...] = n[:HALF]
    second[...] = n[HALF:]


def left_shifted(top, upper, lower, low, above, below, p0, p1, p2, p3, p4, out, y, qh, ql, sems):
    place_left(((0, 0, p0), (3, 0, p1), (1, 0, p2), (2, 0, p3), (2, 64, p4)), qh, ql)

    def q(rows, cols):
        return qh[rows, cols], ql[rows, cols]

    def write(part, k):
        copy = pltpu.make_async_copy(y.at[part], out.at[part], sems.at[k])
        copy.start()
        return copy

    first, second = slice(0, HALF), slice(HALF, WIN)
    a, b, c = slice(0, HALF), slice(HALF, HALF + WIN), slice(HALF + WIN, 2 * WIN)
    y[b, :] = dot3(q(first, b), split(upper[...]), TN) + dot3(q(second, b), split(lower[...]), TN)
    writes = [write(b, 0)]
    y[a, :] = dot3(q(first, a), split(above[...]), TN) + dot3(q(second, a), split(top[...]), TN)
    writes.append(write(a, 1))
    y[c, :] = dot3(q(first, c), split(low[...]), TN) + dot3(q(second, c), split(below[...]), TN)
    writes.append(write(c, 2))
    for copy in writes:
        copy.wait()


LAST = "y"
FLOPS = 3 * 2 * 1024 * 512 * 512
ANY = pl.BlockSpec(memory_space=pl.ANY)
HBM = pl.BlockSpec(memory_space=pltpu.HBM)
VMEM = pl.BlockSpec(memory_space=pltpu.VMEM)
EVERY = slice(None)


def call(kernel, outs, args, specs, scratch, flops, mib, vmem, out_spec=VMEM):
    return pl.pallas_call(
        kernel,
        out_shape=tuple(jax.ShapeDtypeStruct(s, F32) for s in outs),
        in_specs=specs,
        out_specs=(out_spec,) * len(outs),
        scratch_shapes=scratch,
        compiler_params=pltpu.CompilerParams(vmem_limit_bytes=vmem * 2**20),
        cost_estimate=pl.CostEstimate(flops=flops, bytes_accessed=mib * 2**20, transcendentals=0),
    )(*args)


def joined(outs, args, copies, after=()):
    n, m = len(args), len(after)

    def kernel(*refs):
        for source, part, target, place in copies:
            refs[n + m + target][place] = refs[source][part]

    return call(kernel, outs, (*args, *after), [VMEM] * n + [ANY] * m, [], 0, 1, 4)


def stacked(pieces, after=()):
    size, width = pieces[0].shape
    copies = [
        (k, (EVERY, EVERY), 0, (slice(k * size, (k + 1) * size), EVERY)) for k in range(len(pieces))
    ]
    return joined([(len(pieces) * size, width)], pieces, copies, after)[0]


def first_right(schur, pieces, after):
    shape = schur.shape
    half = (shape[0], HALF)
    scratch = [pltpu.VMEM(shape, F32)] + [pltpu.VMEM((WIN, WIN), BF16)] * 2
    scratch.append(pltpu.SemaphoreType.DMA((4,)))
    specs = [HBM] + [VMEM] * 2 + [ANY] * len(after)
    return call(right_aligned, [half, half], (schur, *pieces, *after), specs, scratch, FLOPS, 5, 12)


def prepared(parts, r2, near):
    args = (*parts, *r2, *near)
    outs = [((2 * WIN, WIN), F32)] + [((HALF, WIN), BF16)] * 2 + [((WIN, 2 * WIN), BF16)] * 2
    return pl.pallas_call(
        prepare,
        out_shape=tuple(jax.ShapeDtypeStruct(*o) for o in outs),
        in_specs=[VMEM] * len(args),
        out_specs=(VMEM,) * len(outs),
        scratch_shapes=[pltpu.VMEM((WIN, WIN), BF16)] * 2,
        compiler_params=pltpu.CompilerParams(vmem_limit_bytes=16 * 2**20),
        cost_estimate=pl.CostEstimate(flops=FLOPS // 2, bytes_accessed=7 * 2**20, transcendentals=0),
    )(*args)


def middle_products(w, parts, ready, far):
    args = (*parts, *ready, *far)
    scratch = [pltpu.VMEM((WIN, WIN), F32)] + [pltpu.VMEM((WIN, WIN), BF16)] * 2
    kernel = functools.partial(middle, w)
    return call(kernel, [(HALF, WIN)] * 2, args, [VMEM] * len(args), scratch, 3 * FLOPS // 4, 5, 20)


def last_left(parts, l2):
    scratch = [pltpu.VMEM((2 * WIN, WIN), F32)] + [pltpu.VMEM((WIN, 2 * WIN), BF16)] * 2
    scratch.append(pltpu.SemaphoreType.DMA((3,)))
    args = (*parts, *l2)
    outs = [(2 * WIN, WIN)]
    return call(left_shifted, outs, args, [VMEM] * len(args), scratch, FLOPS, 7, 20, HBM)[0]


def across_next(x):
    rows, cols = lax.axis_size("row"), lax.axis_size("col")
    perm = [(r * cols + c, (r ^ 2) * cols + (c - 1) % cols) for r in range(rows) for c in range(cols)]
    return lax.ppermute(x, ("row", "col"), perm)


def gathered(x):
    size = 8
    groups = [[z * size + i for i in range(size)] for z in range(lax.axis_size("col") // size)]
    copies = jnp.broadcast_to(x[None], (size,) + x.shape)
    out = lax.all_to_all(copies, "col", 0, 0, axis_index_groups=groups)
    return out.reshape(size * x.shape[0], x.shape[1])


def ring(x, to):
    perm = [(i, to(i)) for i in range(lax.axis_size("col"))]
    return lax.ppermute(x, "col", perm)


def along_z(by):
    return lambda i: (i + 8 * by) % 32


def around(x, along):
    up = ring(x, along(1))
    down = ring(x, along(-1))
    return x, up, down, ring(up[:64], along(1)), ring(down[64:], along(-1))


def body(schur, left_rot, right_rot, left_off, right_off):
    l1 = gathered(jnp.concatenate([left_rot[0], left_rot[1]], axis=1))
    l1 = l1, ring(l1, along_z(1)), ring(l1, along_z(-1))
    right_next = right_off[0, :, :HALF]
    right_next = stacked([shift(right_next, "col", -1), across_next(right_next)])
    away = shift(left_off[0, :, :HALF], "row", -1)
    l2 = jnp.concatenate([left_off[0, :, HALF:], left_off[1]], axis=1)
    (l2,) = joined(
        [(16, 2 * WIN)],
        [l2, away],
        [
            (0, (EVERY, EVERY), 0, (EVERY, slice(0, 2 * WIN - HALF))),
            (1, (EVERY, EVERY), 0, (EVERY, slice(2 * WIN - HALF, 2 * WIN))),
        ],
        after=(right_next,),
    )
    l2 = gathered(l2)
    right = jnp.concatenate([right_rot[0], right_off[0, :, HALF:]], axis=1)
    right = stacked([right, swap(right, "row", 2)])
    right_core = swap(right, "row", 1)
    ml, mr = first_right(schur, (right, right_core), (l2, l1[1], l1[2]))
    hl = shift(mr, "col", 1)
    hr = shift(ml, "col", -1)
    next_core = swap(right_next, "row", 1)
    ready = prepared((ml, mr), (right, right_core, right_next, next_core), l1[:3])
    far_first, far_second = joined(
        [(64, 2 * WIN)] * 2,
        [l1[1], l1[2]],
        [(k, (slice(k * 64, k * 64 + 64), EVERY), k, (EVERY, EVERY)) for k in (0, 1)],
        after=(ready[0],),
    )
    far = ring(far_first, along_z(1)), ring(far_second, along_z(-1))
    top, upper = middle_products(0, (hl, hr), ready, far)
    lower, low = middle_products(1, (hl, hr), ready, far)
    l2 = around(l2, along_z)
    above = shift(low, "row", 1)
    below = shift(top, "row", -1)
    return last_left((top, upper, lower, low, above, below), l2)


def solution(mesh):
    return jax.shard_map(
        body,
        mesh=mesh,
        in_specs=(
            P("row", "col"),
            P("row", "col", None),
            P("col", "row", None),
            P("row", "col", None),
            P("col", "row", None),
        ),
        out_specs=P("row", "col"),
        check_vma=False,
    )
```
